32 devices in a mesh: rows: 8 (over z, x), cols: 4 (over y, core).
Axes of the slice: x: 2, y: 2, z: 4, core: 2. Of those that a mesh axis runs over, the one named last changes fastest.
Arguments:
- trailing: float32 [8192, 4096], P('rows', 'cols'), may hold values from -6 to 6
- leaf_v: float32 [8192, 512], P('rows', 'cols'), may hold values from -0.1875 to 0.1875
- leaf_t: float32 [4096, 512], P('rows', 'cols'), may hold values from -0.25 to 0.25
- merge_v: float32 [8192, 512], P('rows'), may hold values from -0.1875 to 0.1875
- merge_t: float32 [4096, 512], P('rows'), may hold values from -0.25 to 0.25
Outputs:
- updated: float32 [8192, 4096], P('rows', 'cols')
The draws below stay inside these ranges and needn't reach their ends.
All inputs are finite; a program needn't handle non-finite values.
Results may differ from the reference program's by a relative error of at most 0.00011.
Values sent between devices are 32-bit elements; how exact they have to be, the bound alone decides.
A program may use at most 128 MiB of HBM per device.

```python
import jax
import jax.numpy as jnp
import numpy as np
from jax import lax

PANEL = 512
ROWS_DEV = 1024
NROWS_ALL = 8192
NCOLS_ALL = 4096
LEVELS = 3
N_ROWS = 8


def block_levels(rng, shape, pieces, low, largest):
    factor_of = 1.0
    for position, parts in pieces:
        draws = jax.random.uniform(jax.random.fold_in(jax.random.fold_in(rng, 6), position), (parts,), jnp.float32, low / len(pieces), largest / len(pieces))
        factor_of = factor_of * jnp.repeat(jnp.exp(draws), shape[position] // parts).reshape((-1,) + (1,) * (len(shape) - 1 - position))
    return factor_of


def scatter_about(rng, dims, deviation, limit, shards=(), dtype=jnp.bfloat16):
    gain = block_levels(rng, dims, shards, -0.22, 0.18) if shards else 1.0
    values = jax.random.normal(rng, dims, jnp.float32) * deviation * gain
    return jnp.minimum(jnp.maximum(values, -limit), limit).astype(dtype)


def setup_inputs(seed: int = 0) -> dict:
    streams_of = jax.random.split(jax.random.key(seed), 6)
    trailing = scatter_about(streams_of[0], (NROWS_ALL, NCOLS_ALL), 1.0, 6.0, ((0, 8), (1, 4)), jnp.float32)
    leaf_v = scatter_about(streams_of[1], (NROWS_ALL, PANEL), ROWS_DEV ** -0.5, 0.1875, ((0, 8), (1, 4)), jnp.float32)
    leaf_t = scatter_about(streams_of[2], (N_ROWS * PANEL, PANEL), PANEL ** -0.5, 0.25, ((0, 8), (1, 4)), jnp.float32)
    merge_v = scatter_about(streams_of[3], (N_ROWS * 2 * PANEL, PANEL), (2 * PANEL) ** -0.5, 0.1875, ((0, 8),), jnp.float32)
    merge_t = scatter_about(streams_of[4], (N_ROWS * PANEL, PANEL), PANEL ** -0.5, 0.25, ((0, 8),), jnp.float32)
    return {"trailing": trailing, "leaf_v": leaf_v, "leaf_t": leaf_t, "merge_v": merge_v, "merge_t": merge_t}


def reference(trailing, leaf_v, leaf_t, merge_v, merge_t):
    highest = lax.Precision.HIGHEST
    blocks = trailing.reshape(N_ROWS, ROWS_DEV, -1)
    vectors = leaf_v.reshape(N_ROWS, ROWS_DEV, PANEL)
    triangles = jnp.triu(leaf_t.reshape(N_ROWS, PANEL, PANEL))
    projected = jnp.einsum('nrk,nrc->nkc', vectors, blocks, precision=highest)
    weights = jnp.einsum('njk,njc->nkc', triangles, projected, precision=highest)
    blocks = blocks - jnp.einsum('nrk,nkc->nrc', vectors, weights, precision=highest)
    tops = blocks[:, :PANEL]
    remains = blocks[:, PANEL:]
    merge_vec = merge_v.reshape(N_ROWS, 2 * PANEL, PANEL)
    merge_tri = jnp.triu(merge_t.reshape(N_ROWS, PANEL, PANEL))
    for level in range(LEVELS):
        stride = 2 ** level
        uppers = np.arange(stride, N_ROWS, 2 * stride)
        lowers = uppers - stride
        upper_a = merge_vec[uppers, :PANEL]
        upper_b = merge_vec[uppers, PANEL:]
        factor = merge_tri[uppers]
        top_low = tops[lowers]
        top_up = tops[uppers]
        summed = jnp.einsum('njk,njc->nkc', upper_a, top_low, precision=highest) + jnp.einsum('njk,njc->nkc', upper_b, top_up, precision=highest)
        weight = jnp.einsum('njk,njc->nkc', factor, summed, precision=highest)
        new_low = top_low - jnp.einsum('njk,nkc->njc', upper_a, weight, precision=highest)
        new_up = top_up - jnp.einsum('njk,nkc->njc', upper_b, weight, precision=highest)
        tops = tops.at[lowers].set(new_low).at[uppers].set(new_up)
    return jnp.concatenate([tops, remains], axis=1).reshape(N_ROWS * ROWS_DEV, -1)
```

```python
import functools

import jax
import jax.numpy as jnp
from jax import lax
from jax.experimental import pallas as pl
from jax.experimental.pallas import tpu as pltpu
from jax.sharding import PartitionSpec as P

F32 = jnp.float32
BF16 = jnp.bfloat16
MESH = pl.DeviceIdType.MESH
CHUNKS = 2


def split(x):
    high = x.astype(BF16)
    return high, (x - high.astype(F32)).astype(BF16)


def dot(a, b):
    return lax.dot_general(a, b, (((1,), (0,)), ((), ())), preferred_element_type=F32)


def mult(ah, al, x):
    bh, bl = split(x)
    return dot(ah, bh) + (dot(ah, bl) + dot(al, bh))


def triu(x):
    row = lax.broadcasted_iota(jnp.int32, x.shape, 0)
    col = lax.broadcasted_iota(jnp.int32, x.shape, 1)
    return jnp.where(row <= col, x, 0.0)


def kernel(nr, tr, lv, lt, mv, mt, out, vb, tb, cb, ab, m0, mg, ml, buf, snd, pk, xs, ys,
           vt, vs, ltt, at, an, m0t, gt, gn, mlt,
           loc, gs, gr, ps, xsend, xrecv, lsend, lrecv, rsend, rrecv):
    levels = nr.bit_length() - 1
    m, p = vb.shape
    n = cb.shape[1]
    half = n // 2
    tc = half // CHUNKS
    tiles = 2 * CHUNKS
    q = lv.shape[1]
    r = lax.axis_index("rows")
    c = lax.axis_index("cols")
    par = r % 2
    mate = r + 1 - 2 * par
    yc = c + 2 - 4 * (c // 2)
    cc = c + 1 - 2 * (c % 2)

    barrier = pltpu.get_barrier_semaphore()
    for step in range(1, nr):
        pl.semaphore_signal(barrier, inc=1, device_id=((r + step) % nr, c), device_id_type=MESH)
    for col in (yc, cc):
        pl.semaphore_signal(barrier, inc=1, device_id=(r, col), device_id_type=MESH)

    def remote(src, dst, send, recv, row, col):
        return pltpu.make_async_remote_copy(src_ref=src, dst_ref=dst, send_sem=send, recv_sem=recv,
                                            device_id=(row, col), device_id_type=MESH)

    def cols_of(k):
        return pl.ds(pl.multiple_of(k * q, q), q)

    items = [lambda k: vb.at[:, cols_of(k)], lambda k: tb.at[:, cols_of(k)],
             lambda k: ab.at[:, cols_of(k)], lambda k: m0.at[cols_of(k)]]
    for l in range(1, levels):
        items.append(functools.partial(lambda l, k: mg.at[l - 1, cols_of(k)], l))
        items.append(functools.partial(lambda l, k: ml.at[l - 1, cols_of(k)], l))

    def y_copy(i, src=None):
        return remote(items[i](c) if src is None else src, items[i](c), gs.at[i, 0], gr.at[i, 0], r, yc)

    def own_copy(i, src=None):
        return remote(items[i](c) if src is None else src, items[i](c), gs.at[i, 1], gr.at[i, 1], r, cc)

    def fwd_copy(i):
        return remote(items[i](yc), items[i](yc), gs.at[i, 2], gr.at[i, 2], r, cc)

    def in_wait(i):
        remote(items[i](c), items[i](c), gs.at[i, 0], gr.at[i, 3], r, c).wait_recv()

    def forward(i):
        y_copy(i).wait_recv()
        fwd_copy(i).start()

    def stride(l):
        return 1 << l

    def active(l):
        return r % stride(l) < 2

    def upper(l):
        return (r // stride(l)) % 2 == 1

    def holder(l):
        return r % stride(l + 1) == stride(l)

    def needs(l):
        return jnp.logical_and(active(l), jnp.logical_not(holder(l)))

    trail_in = pltpu.make_async_copy(tr, cb, loc.at[0])
    v_in = pltpu.make_async_copy(lv, items[0](c), loc.at[1])
    t_in = pltpu.make_async_copy(lt, items[1](c), loc.at[2])
    v_in.start()
    trail_in.start()
    t_in.start()
    ab_in = pltpu.make_async_copy(mv, ab, loc.at[3])
    m_in = pltpu.make_async_copy(mt, m0, loc.at[4])

    pl.semaphore_wait(barrier, nr + 1)
    own_copy(0, lv).start()
    y_copy(0, lv).start()
    own_copy(1, lt).start()
    y_copy(1, lt).start()

    def first_sends():
        return [remote(mv.at[:, cols_of(c)], ab.at[:, cols_of(c)], ps.at[0, 0], gr.at[2, 3], mate, c),
                remote(mt.at[cols_of(c)], m0.at[cols_of(c)], ps.at[0, 1], gr.at[3, 3], mate, c)]

    def level_sends(l):
        i = 2 + 2 * l
        sends = []
        for k, (row, side) in enumerate(((r - stride(l), 0), (r - stride(l) + 1, 0), (r + 1, 1))):
            sends.append(remote(mv.at[side, cols_of(c)], mg.at[l - 1, cols_of(c)],
                                ps.at[l, 2 * k], gr.at[i, 3], row, c))
            sends.append(remote(mt.at[cols_of(c)], ml.at[l - 1, cols_of(c)],
                                ps.at[l, 2 * k + 1], gr.at[i + 1, 3], row, c))
        return sends

    def own_level(l):
        return [pltpu.make_async_copy(mv.at[1], mg.at[l - 1], loc.at[3]),
                pltpu.make_async_copy(mt, ml.at[l - 1], loc.at[4])]

    @pl.when(par == 1)
    def _():
        for copy in first_sends():
            copy.start()
        ab_in.start()
        m_in.start()

    for l in range(1, levels):
        @pl.when(holder(l))
        def _(l=l):
            for copy in level_sends(l) + own_level(l):
                copy.start()

    def place(s):
        sent = s < CHUNKS
        chunk = jnp.where(sent, s, s - CHUNKS)
        side = jnp.where(sent, 1 - par, par)
        return pl.ds(pl.multiple_of(side * half + chunk * tc, tc), tc)

    def project(block):
        rows = pl.ds(pl.multiple_of(block * 2 * q, 2 * q), 2 * q)
        piece = vb[:, rows]
        high, low = split(piece)
        vs[0, :, rows] = high
        vs[1, :, rows] = low
        high, low = split(piece.T)
        vt[0, rows] = high
        vt[1, rows] = low

        def body(s, _):
            pk[s, rows] = mult(vt[0, rows], vt[1, rows], cb[:, place(s)])
            return 0

        lax.fori_loop(0, tiles, body, 0)

    v_in.wait()
    own_copy(0).wait_recv()
    trail_in.wait()
    project(c // 2)
    forward(0)
    fwd_copy(0).wait_recv()
    project(1 - c // 2)
    forward(1)

    @pl.when(par == 0)
    def _():
        for i in (2, 3):
            in_wait(i)
            y_copy(i).start()
            own_copy(i).start()

    t_in.wait()
    own_copy(1).wait_recv()
    fwd_copy(1).wait_recv()
    high, low = split(triu(tb[...]).T)
    ltt[0] = high
    ltt[1] = low

    def swap(ch):
        return remote(snd.at[ch], buf.at[par, ch], lsend.at[ch], lrecv.at[ch], mate, c)

    def leaf(s, dest):
        weights = mult(ltt[0], ltt[1], pk[s])
        pk[s] = weights
        dest[...] = cb[:p, place(s)] - mult(vs[0, :p], vs[1, :p], weights)

    def leaf_sent(ch, _):
        leaf(ch, snd.at[ch])
        swap(ch).start()
        return 0

    def leaf_kept(ch, _):
        leaf(ch + CHUNKS, buf.at[par, ch])
        return 0

    lax.fori_loop(0, CHUNKS, leaf_sent, 0)
    lax.fori_loop(0, CHUNKS, leaf_kept, 0)

    @pl.when(par == 0)
    def _():
        forward(2)
        forward(3)

    for l in range(1, levels):
        @pl.when(needs(l))
        def _(l=l):
            for i in (2 + 2 * l, 3 + 2 * l):
                in_wait(i)
                y_copy(i).start()
                own_copy(i).start()

    def remains(s, _):
        cb[p:, place(s)] = cb[p:, place(s)] - mult(vs[0, p:], vs[1, p:], pk[s])
        return 0

    lax.fori_loop(0, tiles, remains, 0)
    rest_out = pltpu.make_async_copy(cb.at[pl.ds(p, m - p)], out.at[pl.ds(p, m - p)], loc.at[0])
    rest_out.start()

    @pl.when(par == 0)
    def _():
        for i in (2, 3):
            own_copy(i).wait_recv()
            fwd_copy(i).wait_recv()

    @pl.when(par == 1)
    def _():
        ab_in.wait()
        m_in.wait()

    def prepare(k, _):
        an[k, 0], an[k, 1] = split(ab[k])
        at[k, 0], at[k, 1] = split(ab[k].T)
        return 0

    lax.fori_loop(0, 2, prepare, 0)
    m0t[0], m0t[1] = split(triu(m0[...]).T)

    def level_ready(l):
        @pl.when(needs(l))
        def _():
            for i in (2 + 2 * l, 3 + 2 * l):
                forward(i)
            for i in (2 + 2 * l, 3 + 2 * l):
                own_copy(i).wait_recv()
                fwd_copy(i).wait_recv()

        @pl.when(holder(l))
        def _():
            for copy in own_level(l):
                copy.wait()

        @pl.when(active(l))
        def _():
            gn[l - 1, 0], gn[l - 1, 1] = split(mg[l - 1])
            gt[l - 1, 0], gt[l - 1, 1] = split(mg[l - 1].T)
            mlt[l - 1, 0], mlt[l - 1, 1] = split(triu(ml[l - 1]).T)

    def exchange(l, ch):
        partner = r + stride(l) - 2 * stride(l) * ((r // stride(l)) % 2)
        return remote(xs.at[l - 1, ch], ys.at[l - 1, ch], xsend.at[l - 1, ch], xrecv.at[l - 1, ch], partner, c)

    def out_of(side, ch):
        return out.at[pl.ds(0, p), pl.ds(pl.multiple_of(side * half + ch * tc, tc), tc)]

    def give(k, ch):
        return remote(buf.at[k, ch], out_of(1 - k, ch), rsend.at[k, ch], rrecv.at[k, ch], mate, c)

    def keep(k, ch):
        return pltpu.make_async_copy(buf.at[k, ch], out_of(k, ch), rsend.at[k, ch])

    def finish(k, ch):
        @pl.when(par == k)
        def _():
            keep(k, ch).start()

        @pl.when(par != k)
        def _():
            give(k, ch).start()

    def leave(l, ch):
        if l == levels:
            finish(0, ch)
            return

        @pl.when(active(l))
        def _():
            xs[l - 1, ch] = mult(gt[l - 1, 0], gt[l - 1, 1], buf[0, ch])
            exchange(l, ch).start()

    def first(ch, _):
        swap(ch).wait_recv()
        total = mult(at[0, 0], at[0, 1], buf[0, ch]) + mult(at[1, 0], at[1, 1], buf[1, ch])
        weights = mult(m0t[0], m0t[1], total)
        wh, wl = split(weights)
        for k in (1, 0):
            high, low = an[k, 0], an[k, 1]
            buf[k, ch] = buf[k, ch] - (dot(high, wh) + (dot(high, wl) + dot(low, wh)))
            if k:
                finish(1, ch)
        leave(1, ch)
        return 0

    if levels > 1:
        level_ready(1)
    lax.fori_loop(0, CHUNKS, first, 0)

    for l in range(1, levels):
        if l + 1 < levels:
            level_ready(l + 1)

        def merge(ch, _, l=l):
            exchange(l, ch).wait_recv()
            weights = mult(mlt[l - 1, 0], mlt[l - 1, 1], xs[l - 1, ch] + ys[l - 1, ch])
            buf[0, ch] = buf[0, ch] - mult(gn[l - 1, 0], gn[l - 1, 1], weights)

            @pl.when(upper(l))
            def _():
                finish(0, ch)

            @pl.when(jnp.logical_not(upper(l)))
            def _():
                leave(l + 1, ch)
            return 0

        @pl.when(active(l))
        def _(merge=merge):
            lax.fori_loop(0, CHUNKS, merge, 0)

    rest_out.wait()
    for i in (0, 1):
        y_copy(i).wait_send()
        own_copy(i).wait_send()
        fwd_copy(i).wait_send()

    @pl.when(par == 1)
    def _():
        for copy in first_sends():
            copy.wait_send()

    @pl.when(par == 0)
    def _():
        for i in (2, 3):
            y_copy(i).wait_send()
            own_copy(i).wait_send()
            fwd_copy(i).wait_send()

    for l in range(1, levels):
        @pl.when(holder(l))
        def _(l=l):
            for copy in level_sends(l):
                copy.wait_send()

        @pl.when(needs(l))
        def _(l=l):
            for i in (2 + 2 * l, 3 + 2 * l):
                y_copy(i).wait_send()
                own_copy(i).wait_send()
                fwd_copy(i).wait_send()

        @pl.when(active(l))
        def _(l=l):
            for ch in range(CHUNKS):
                exchange(l, ch).wait_send()

    for ch in range(CHUNKS):
        swap(ch).wait_send()
        for k in (0, 1):
            @pl.when(par == k)
            def _(k=k, ch=ch):
                keep(k, ch).wait()
                remote(buf.at[k, ch], out_of(1 - k, ch), rsend.at[k, ch], rrecv.at[k, ch], mate, c).wait_recv()

            @pl.when(par != k)
            def _(k=k, ch=ch):
                give(k, ch).wait_send()


def on_device(nr, nc, trailing, leaf_v, leaf_t, merge_v, merge_t):
    m, n = trailing.shape
    p = merge_t.shape[1]
    levels = nr.bit_length() - 1
    more = max(levels - 1, 1)
    tc = n // 2 // CHUNKS
    n_items = 2 + 2 * levels
    assert nc == 4 and nr == 1 << levels and levels > 0
    vmem = pltpu.VMEM
    sem = pltpu.SemaphoreType.DMA
    call = pl.pallas_call(
        functools.partial(kernel, nr),
        out_shape=jax.ShapeDtypeStruct((m, n), F32),
        in_specs=[pl.BlockSpec(memory_space=pl.ANY)] * 5,
        out_specs=pl.BlockSpec(memory_space=pl.ANY),
        scratch_shapes=[
            vmem((m, p), F32), vmem((p, p), F32), vmem((m, n), F32),
            vmem((2, p, p), F32), vmem((p, p), F32),
            vmem((more, p, p), F32), vmem((more, p, p), F32),
            vmem((2, CHUNKS, p, tc), F32), vmem((CHUNKS, p, tc), F32),
            vmem((2 * CHUNKS, p, tc), F32),
            vmem((more, CHUNKS, p, tc), F32), vmem((more, CHUNKS, p, tc), F32),
            vmem((2, p, m), BF16), vmem((2, m, p), BF16), vmem((2, p, p), BF16),
            vmem((2, 2, p, p), BF16), vmem((2, 2, p, p), BF16), vmem((2, p, p), BF16),
            vmem((more, 2, p, p), BF16), vmem((more, 2, p, p), BF16), vmem((more, 2, p, p), BF16),
            sem((5,)), sem((n_items, 3)), sem((n_items, 4)), sem((levels, 6)),
            sem((more, CHUNKS)), sem((more, CHUNKS)), sem((CHUNKS,)), sem((CHUNKS,)),
            sem((2, CHUNKS)), sem((2, CHUNKS)),
        ],
        compiler_params=pltpu.CompilerParams(
            collective_id=0, has_side_effects=True, vmem_limit_bytes=60 << 20),
        cost_estimate=pl.CostEstimate(
            flops=2 * n * p * (3 * m + 3 * p * levels), bytes_accessed=4 * (2 * m * n + 4 * m * p), transcendentals=0),
    )
    return call(trailing, leaf_v, leaf_t, merge_v.reshape(2, p, p), merge_t)


def solution(mesh):
    return jax.shard_map(
        functools.partial(on_device, mesh.shape["rows"], mesh.shape["cols"]),
        mesh=mesh,
        in_specs=(
            P("rows", "cols"),
            P("rows", "cols"),
            P("rows", "cols"),
            P("rows", None),
            P("rows", None),
        ),
        out_specs=P("rows", "cols"),
        check_vma=False,
    )
```

```python
import functools

import jax
import jax.numpy as jnp
from jax import lax
from jax.experimental import pallas as pl
from jax.experimental.pallas import tpu as pltpu
from jax.sharding import PartitionSpec as P

F32 = jnp.float32
BF16 = jnp.bfloat16
MESH = pl.DeviceIdType.MESH
CHUNKS = 4
WIDE = 2


def split(x):
    high = x.astype(BF16)
    return high, (x - high.astype(F32)).astype(BF16)


def dot(a, b):
    return lax.dot_general(a, b, (((1,), (0,)), ((), ())), preferred_element_type=F32)


def mult(ah, al, x):
    bh, bl = split(x)
    return dot(ah, bh) + (dot(ah, bl) + dot(al, bh))


def triu(x):
    row = lax.broadcasted_iota(jnp.int32, x.shape, 0)
    col = lax.broadcasted_iota(jnp.int32, x.shape, 1)
    return jnp.where(row <= col, x, 0.0)


def kernel(nr, tr, lv, lt, mv, mt, out, vb, tb, cb, ab, m0, mg, ml, buf, snd, pk, xs, ys,
           vt, vs, ltt, at, an, m0t, gt, gn, mlt,
           loc, gs, gr, ps, xsend, xrecv, lsend, lrecv, rsend, rrecv):
    levels = nr.bit_length() - 1
    m, p = vb.shape
    n = cb.shape[1]
    half = n // 2
    tc = half // CHUNKS
    tw = tc * WIDE
    tiles = n // tw
    q = lv.shape[1]
    r = lax.axis_index("rows")
    c = lax.axis_index("cols")
    par = r % 2
    mate = r + 1 - 2 * par
    yc = c + 2 - 4 * (c // 2)
    cc = c + 1 - 2 * (c % 2)

    barrier = pltpu.get_barrier_semaphore()
    for step in range(1, nr):
        pl.semaphore_signal(barrier, inc=1, device_id=((r + step) % nr, c), device_id_type=MESH)
    for col in (yc, cc):
        pl.semaphore_signal(barrier, inc=1, device_id=(r, col), device_id_type=MESH)

    def remote(src, dst, send, recv, row, col):
        return pltpu.make_async_remote_copy(src_ref=src, dst_ref=dst, send_sem=send, recv_sem=recv,
                                            device_id=(row, col), device_id_type=MESH)

    def cols_of(k):
        return pl.ds(pl.multiple_of(k * q, q), q)

    items = [lambda k: vb.at[:, cols_of(k)], lambda k: tb.at[:, cols_of(k)],
             lambda k: ab.at[:, cols_of(k)], lambda k: m0.at[cols_of(k)]]
    for l in range(1, levels):
        items.append(functools.partial(lambda l, k: mg.at[l - 1, cols_of(k)], l))
        items.append(functools.partial(lambda l, k: ml.at[l - 1, cols_of(k)], l))

    def y_copy(i, src=None):
        return remote(items[i](c) if src is None else src, items[i](c), gs.at[i, 0], gr.at[i, 0], r, yc)

    def own_copy(i, src=None):
        return remote(items[i](c) if src is None else src, items[i](c), gs.at[i, 1], gr.at[i, 1], r, cc)

    def fwd_copy(i):
        return remote(items[i](yc), items[i](yc), gs.at[i, 2], gr.at[i, 2], r, cc)

    def in_wait(i):
        remote(items[i](c), items[i](c), gs.at[i, 0], gr.at[i, 3], r, c).wait_recv()

    def forward(i):
        y_copy(i).wait_recv()
        fwd_copy(i).start()

    def stride(l):
        return 1 << l

    def active(l):
        return r % stride(l) < 2

    def upper(l):
        return (r // stride(l)) % 2 == 1

    def holder(l):
        return r % stride(l + 1) == stride(l)

    def needs(l):
        return jnp.logical_and(active(l), jnp.logical_not(holder(l)))

    trail_in = pltpu.make_async_copy(tr, cb, loc.at[0])
    v_in = pltpu.make_async_copy(lv, items[0](c), loc.at[1])
    t_in = pltpu.make_async_copy(lt, items[1](c), loc.at[2])
    v_in.start()
    trail_in.start()
    t_in.start()
    ab_in = pltpu.make_async_copy(mv, ab, loc.at[3])
    m_in = pltpu.make_async_copy(mt, m0, loc.at[4])

    pl.semaphore_wait(barrier, nr + 1)
    own_copy(0, lv).start()
    y_copy(0, lv).start()
    own_copy(1, lt).start()
    y_copy(1, lt).start()

    def first_sends():
        return [remote(mv.at[:, cols_of(c)], ab.at[:, cols_of(c)], ps.at[0, 0], gr.at[2, 3], mate, c),
                remote(mt.at[cols_of(c)], m0.at[cols_of(c)], ps.at[0, 1], gr.at[3, 3], mate, c)]

    def level_sends(l):
        i = 2 + 2 * l
        sends = []
        for k, (row, side) in enumerate(((r - stride(l), 0), (r - stride(l) + 1, 0), (r + 1, 1))):
            sends.append(remote(mv.at[side, cols_of(c)], mg.at[l - 1, cols_of(c)],
                                ps.at[l, 2 * k], gr.at[i, 3], row, c))
            sends.append(remote(mt.at[cols_of(c)], ml.at[l - 1, cols_of(c)],
                                ps.at[l, 2 * k + 1], gr.at[i + 1, 3], row, c))
        return sends

    def own_level(l, which):
        if which == 0:
            return pltpu.make_async_copy(mv.at[1], mg.at[l - 1], loc.at[3])
        return pltpu.make_async_copy(mt, ml.at[l - 1], loc.at[4])

    @pl.when(par == 1)
    def _():
        for copy in first_sends():
            copy.start()
        ab_in.start()
        m_in.start()

    for l in range(1, levels):
        @pl.when(holder(l))
        def _(l=l):
            for copy in level_sends(l) + [own_level(l, 0), own_level(l, 1)]:
                copy.start()

    def place(s):
        sent = s < tiles // 2
        tile = jnp.where(sent, s, s - tiles // 2)
        side = jnp.where(sent, 1 - par, par)
        return pl.ds(pl.multiple_of(side * half + tile * tw, tw), tw)

    def project(block):
        rows = pl.ds(pl.multiple_of(block * 2 * q, 2 * q), 2 * q)
        piece = vb[:, rows]
        high, low = split(piece)
        vs[0, :, rows] = high
        vs[1, :, rows] = low
        high, low = split(piece.T)
        vt[0, rows] = high
        vt[1, rows] = low

        def body(s, _):
            pk[s, rows] = mult(vt[0, rows], vt[1, rows], cb[:, place(s)])
            return 0

        lax.fori_loop(0, tiles, body, 0)

    v_in.wait()
    own_copy(0).wait_recv()
    trail_in.wait()
    project(c // 2)
    forward(0)
    fwd_copy(0).wait_recv()
    project(1 - c // 2)
    forward(1)

    @pl.when(par == 0)
    def _():
        for i in (2, 3):
            in_wait(i)
            y_copy(i).start()
            own_copy(i).start()

    t_in.wait()
    own_copy(1).wait_recv()
    fwd_copy(1).wait_recv()
    high, low = split(triu(tb[...]).T)
    ltt[0] = high
    ltt[1] = low

    def swap(ch):
        return remote(snd.at[ch], buf.at[par, ch], lsend.at[ch], lrecv.at[ch], mate, c)

    def leaf(s):
        weights = mult(ltt[0], ltt[1], pk[s])
        pk[s] = weights
        return cb[:p, place(s)] - mult(vs[0, :p], vs[1, :p], weights)

    def leaf_sent(t, _):
        top = leaf(t)
        for k in range(WIDE):
            snd[t * WIDE + k] = top[:, k * tc:(k + 1) * tc]
            swap(t * WIDE + k).start()
        return 0

    def leaf_kept(t, _):
        top = leaf(t + tiles // 2)
        for k in range(WIDE):
            buf[par, t * WIDE + k] = top[:, k * tc:(k + 1) * tc]
        return 0

    lax.fori_loop(0, tiles // 2, leaf_sent, 0)
    lax.fori_loop(0, tiles // 2, leaf_kept, 0)

    @pl.when(par == 0)
    def _():
        forward(2)
        forward(3)

    for l in range(1, levels):
        @pl.when(needs(l))
        def _(l=l):
            for i in (2 + 2 * l, 3 + 2 * l):
                in_wait(i)
                y_copy(i).start()
                own_copy(i).start()

    def remains(s, _):
        cb[p:, place(s)] = cb[p:, place(s)] - mult(vs[0, p:], vs[1, p:], pk[s])
        return 0

    lax.fori_loop(0, tiles, remains, 0)
    rest_out = pltpu.make_async_copy(cb.at[pl.ds(p, m - p)], out.at[pl.ds(p, m - p)], loc.at[0])
    rest_out.start()

    @pl.when(par == 0)
    def _():
        for i in (2, 3):
            own_copy(i).wait_recv()
            fwd_copy(i).wait_recv()

    @pl.when(par == 1)
    def _():
        ab_in.wait()
        m_in.wait()

    def prepare(k, _):
        an[k, 0], an[k, 1] = split(ab[k])
        at[k, 0], at[k, 1] = split(ab[k].T)
        return 0

    lax.fori_loop(0, 2, prepare, 0)
    m0t[0], m0t[1] = split(triu(m0[...]).T)

    def arrived(i, l, which):
        @pl.when(needs(l))
        def _():
            forward(i)
            own_copy(i).wait_recv()
            fwd_copy(i).wait_recv()

        @pl.when(holder(l))
        def _():
            own_level(l, which).wait()

    def vectors_ready(l):
        arrived(2 + 2 * l, l, 0)

        @pl.when(active(l))
        def _():
            gt[l - 1, 0], gt[l - 1, 1] = split(mg[l - 1].T)
            gn[l - 1, 0], gn[l - 1, 1] = split(mg[l - 1])

    def triangle_ready(l):
        arrived(3 + 2 * l, l, 1)

        @pl.when(active(l))
        def _():
            mlt[l - 1, 0], mlt[l - 1, 1] = split(triu(ml[l - 1]).T)

    def exchange(l, ch):
        partner = r + stride(l) - 2 * stride(l) * ((r // stride(l)) % 2)
        return remote(xs.at[l - 1, ch], ys.at[l - 1, ch], xsend.at[l - 1, ch], xrecv.at[l - 1, ch], partner, c)

    def out_of(side, ch):
        return out.at[pl.ds(0, p), pl.ds(pl.multiple_of(side * half + ch * tc, tc), tc)]

    def give(k, ch):
        return remote(buf.at[k, ch], out_of(1 - k, ch), rsend.at[k, ch], rrecv.at[k, ch], mate, c)

    def keep(k, ch):
        return pltpu.make_async_copy(buf.at[k, ch], out_of(k, ch), rsend.at[k, ch])

    def finish(k, ch):
        @pl.when(par == k)
        def _():
            keep(k, ch).start()

        @pl.when(par != k)
        def _():
            give(k, ch).start()

    def leave(l, ch):
        if l == levels:
            finish(0, ch)
            return

        @pl.when(active(l))
        def _():
            xs[l - 1, ch] = mult(gt[l - 1, 0], gt[l - 1, 1], buf[0, ch])
            exchange(l, ch).start()

    def first(ch, _):
        swap(ch).wait_recv()
        total = mult(at[0, 0], at[0, 1], buf[0, ch]) + mult(at[1, 0], at[1, 1], buf[1, ch])
        weights = mult(m0t[0], m0t[1], total)
        wh, wl = split(weights)
        for k in (1, 0):
            high, low = an[k, 0], an[k, 1]
            buf[k, ch] = buf[k, ch] - (dot(high, wh) + (dot(high, wl) + dot(low, wh)))
        leave(1, ch)
        return 0

    if levels > 1:
        vectors_ready(1)
    lax.fori_loop(0, CHUNKS, first, 0)

    def home(ch, _):
        finish(1, ch)
        return 0

    lax.fori_loop(0, CHUNKS, home, 0)

    for l in range(1, levels):
        triangle_ready(l)
        if l + 1 < levels:
            vectors_ready(l + 1)

        def merge(ch, _, l=l):
            exchange(l, ch).wait_recv()
            weights = mult(mlt[l - 1, 0], mlt[l - 1, 1], xs[l - 1, ch] + ys[l - 1, ch])
            buf[0, ch] = buf[0, ch] - mult(gn[l - 1, 0], gn[l - 1, 1], weights)

            @pl.when(upper(l))
            def _():
                finish(0, ch)

            @pl.when(jnp.logical_not(upper(l)))
            def _():
                leave(l + 1, ch)
            return 0

        @pl.when(active(l))
        def _(merge=merge):
            lax.fori_loop(0, CHUNKS, merge, 0)

    rest_out.wait()
    for i in (0, 1):
        y_copy(i).wait_send()
        own_copy(i).wait_send()
        fwd_copy(i).wait_send()

    @pl.when(par == 1)
    def _():
        for copy in first_sends():
            copy.wait_send()

    @pl.when(par == 0)
    def _():
        for i in (2, 3):
            y_copy(i).wait_send()
            own_copy(i).wait_send()
            fwd_copy(i).wait_send()

    for l in range(1, levels):
        @pl.when(holder(l))
        def _(l=l):
            for copy in level_sends(l):
                copy.wait_send()

        @pl.when(needs(l))
        def _(l=l):
            for i in (2 + 2 * l, 3 + 2 * l):
                y_copy(i).wait_send()
                own_copy(i).wait_send()
                fwd_copy(i).wait_send()

        @pl.when(active(l))
        def _(l=l):
            for ch in range(CHUNKS):
                exchange(l, ch).wait_send()

    for ch in range(CHUNKS):
        swap(ch).wait_send()
        for k in (0, 1):
            @pl.when(par == k)
            def _(k=k, ch=ch):
                keep(k, ch).wait()
                remote(buf.at[k, ch], out_of(1 - k, ch), rsend.at[k, ch], rrecv.at[k, ch], mate, c).wait_recv()

            @pl.when(par != k)
            def _(k=k, ch=ch):
                give(k, ch).wait_send()


def on_device(nr, nc, trailing, leaf_v, leaf_t, merge_v, merge_t):
    m, n = trailing.shape
    p = merge_t.shape[1]
    levels = nr.bit_length() - 1
    more = max(levels - 1, 1)
    tc = n // 2 // CHUNKS
    n_items = 2 + 2 * levels
    assert nc == 4 and nr == 1 << levels and levels > 0
    vmem = pltpu.VMEM
    sem = pltpu.SemaphoreType.DMA
    call = pl.pallas_call(
        functools.partial(kernel, nr),
        out_shape=jax.ShapeDtypeStruct((m, n), F32),
        in_specs=[pl.BlockSpec(memory_space=pl.ANY)] * 5,
        out_specs=pl.BlockSpec(memory_space=pl.ANY),
        scratch_shapes=[
            vmem((m, p), F32), vmem((p, p), F32), vmem((m, n), F32),
            vmem((2, p, p), F32), vmem((p, p), F32),
            vmem((more, p, p), F32), vmem((more, p, p), F32),
            vmem((2, CHUNKS, p, tc), F32), vmem((CHUNKS, p, tc), F32),
            vmem((n // (WIDE * tc), p, WIDE * tc), F32),
            vmem((more, CHUNKS, p, tc), F32), vmem((more, CHUNKS, p, tc), F32),
            vmem((2, p, m), BF16), vmem((2, m, p), BF16), vmem((2, p, p), BF16),
            vmem((2, 2, p, p), BF16), vmem((2, 2, p, p), BF16), vmem((2, p, p), BF16),
            vmem((more, 2, p, p), BF16), vmem((more, 2, p, p), BF16), vmem((more, 2, p, p), BF16),
            sem((5,)), sem((n_items, 3)), sem((n_items, 4)), sem((levels, 6)),
            sem((more, CHUNKS)), sem((more, CHUNKS)), sem((CHUNKS,)), sem((CHUNKS,)),
            sem((2, CHUNKS)), sem((2, CHUNKS)),
        ],
        compiler_params=pltpu.CompilerParams(
            collective_id=0, has_side_effects=True, vmem_limit_bytes=60 << 20),
        cost_estimate=pl.CostEstimate(
            flops=2 * n * p * (3 * m + 3 * p * levels), bytes_accessed=4 * (2 * m * n + 4 * m * p), transcendentals=0),
    )
    return call(trailing, leaf_v, leaf_t, merge_v.reshape(2, p, p), merge_t)


def solution(mesh):
    return jax.shard_map(
        functools.partial(on_device, mesh.shape["rows"], mesh.shape["cols"]),
        mesh=mesh,
        in_specs=(
            P("rows", "cols"),
            P("rows", "cols"),
            P("rows", "cols"),
            P("rows", None),
            P("rows", None),
        ),
        out_specs=P("rows", "cols"),
        check_vma=False,
    )
```
